256 devices in a mesh: ctx: 64 (over z, x, core), tp: 4 (over y).
Axes of the slice: x: 4, y: 4, z: 8, core: 2. Of those that a mesh axis runs over, the one named last changes fastest.
Arguments:
- queries: bfloat16 [8192, 3072], P('ctx', 'tp'), may hold values from -70 to 70
- keys: bfloat16 [8192, 512], P('ctx', 'tp'), may hold values from -6 to 6
- values: bfloat16 [8192, 512], P('ctx', 'tp'), may hold values from -6 to 6
- out_grad: bfloat16 [8192, 6144], P('ctx', 'tp'), may hold values from -6 to 6
- out_weight: bfloat16 [3072, 6144], P('tp'), may hold values from -0.078125 to 0.078125
- pair_order: int32 [64], replicated, may hold values from 0 to 63, each once
Outputs:
- query_gradient: float32 [8192, 3072], P('ctx', 'tp')
- grad_keys: float32 [8192, 512], P('ctx', 'tp')
- grad_values: float32 [8192, 512], P('ctx', 'tp')
The draws below stay inside these ranges and needn't reach their ends.
Inputs may be any that keep to these rules, and one draw needn't show every extreme that they name: A permutation: ctx index i holds the spans pair_order[i] and 127 - pair_order[i] of 64 positions, the lower one in its first 64 rows.
All inputs are finite; a program needn't handle non-finite values.
Results may differ from the reference program's by a relative error of at most 0.01.
Values may be sent and summed in bfloat16 or wider, within the bound.
No kernel may reach another device: no remote copies, remote signals or barrier semaphores. Data moves between devices by JAX's collectives and lax.ppermute only.
A program may use at most 64 MiB of HBM per device.

```python
import math
import jax
import jax.numpy as jnp
from jax import lax

D = 6144
QUERY_HEADS = 24
KEY_VALUE_HEADS = 4
HEAD_SIZE = 128
TOK_DEV = 128
SEQUENCE_LENGTH = 8192
PAIRS = 64
SPAN = 64


def draw_keys(key, part):
    key = jax.random.fold_in(key, 3)
    backward_result = jnp.clip(jax.random.normal(key, (SEQUENCE_LENGTH, KEY_VALUE_HEADS * HEAD_SIZE), jnp.float32), -5.5, 5.5)
    return backward_result.astype(jnp.bfloat16)


def draw_queries(key, part):
    key = jax.random.fold_in(key, 5)
    backward_result = jax.random.normal(key, (SEQUENCE_LENGTH, QUERY_HEADS * HEAD_SIZE), jnp.float32)
    return backward_result.astype(jnp.bfloat16)


def block_levels(own_key, extent, cuts, smallest, high):
    factor_of, own = 1.0, jax.random.fold_in(own_key, 6)
    for dim, parts in cuts:
        draws = jnp.exp(jax.random.uniform(jax.random.fold_in(own, dim), (parts,), jnp.float32, smallest / len(cuts), high / len(cuts)))
        factor_of = factor_of * jnp.repeat(draws, extent[dim] // parts).reshape([-1 if axis == dim else 1 for axis in range(len(extent))])
    return factor_of


def normal_values(own_key, dims, width, limit, cuts=(), kind=jnp.bfloat16):
    level = block_levels(own_key, dims, cuts, -0.22, 0.18) if cuts else 1.0
    result = jax.random.normal(own_key, dims, jnp.float32) * width * level
    return jnp.minimum(jnp.maximum(result, -limit), limit).astype(kind)


def setup_inputs(seed: int = 0) -> dict:
    splits = jax.random.split(jax.random.key(seed), 7)
    return {
        "queries": draw_queries(jax.random.fold_in(splits[6], 71), 0),
        "keys": draw_keys(jax.random.fold_in(splits[6], 71), 0),
        "values": normal_values(splits[2], (SEQUENCE_LENGTH, KEY_VALUE_HEADS * HEAD_SIZE), 1.0, 6.0, ((0, 64), (1, 4))),
        "out_grad": normal_values(splits[3], (SEQUENCE_LENGTH, D), 1.0, 6.0, ((0, 64), (1, 4))),
        "out_weight": normal_values(splits[4], (QUERY_HEADS * HEAD_SIZE, D), D ** -0.5, 0.078125, ((0, 4),)),
        "pair_order": jax.random.permutation(splits[5], PAIRS).astype(jnp.int32),
    }


def position_table(pair_order):
    all_rows = jnp.arange(SEQUENCE_LENGTH, dtype=jnp.int32)
    owners = all_rows // TOK_DEV
    local_row = all_rows % TOK_DEV
    pair_ids = pair_order[owners]
    span_ids = jnp.where(local_row < SPAN, pair_ids, 2 * PAIRS - 1 - pair_ids)
    return (span_ids * SPAN + local_row % SPAN).astype(jnp.int32)


def reference(queries, keys, values, out_grad, out_weight, pair_order):
    group_size = QUERY_HEADS // KEY_VALUE_HEADS
    score_scale = HEAD_SIZE ** -0.5
    head_gradient = lax.dot_general(out_grad, out_weight, (((1,), (1,)), ((), ())), preferred_element_type=jnp.float32).astype(jnp.bfloat16)
    positions = position_table(pair_order)
    complete_keys = keys.astype(jnp.float32).reshape(SEQUENCE_LENGTH, KEY_VALUE_HEADS, HEAD_SIZE)
    complete_values = values.astype(jnp.float32).reshape(SEQUENCE_LENGTH, KEY_VALUE_HEADS, HEAD_SIZE)
    block_length = math.gcd(SEQUENCE_LENGTH, 128)
    number_of_blocks = SEQUENCE_LENGTH // block_length
    blocked_queries = queries.reshape(number_of_blocks, block_length, KEY_VALUE_HEADS, group_size, HEAD_SIZE)
    gradient_blocks = head_gradient.reshape(number_of_blocks, block_length, KEY_VALUE_HEADS, group_size, HEAD_SIZE)
    pos_blocks = positions.reshape(number_of_blocks, block_length)

    def advance(folded, inputs):
        key_accumulator, value_accumulator = folded
        query_part, grads_part, query_pos = inputs
        query_float = query_part.astype(jnp.float32)
        grads_float = grads_part.astype(jnp.float32)
        scores = jnp.einsum("qkgd,skd->kgqs", query_float, complete_keys) * score_scale
        allowed = positions[None, :] <= query_pos[:, None]
        scores = jnp.where(allowed[None, None], scores, -jnp.inf)
        largest = jnp.max(scores, axis=3, keepdims=True)
        log_total = largest + jnp.log(jnp.sum(jnp.exp(scores - largest), axis=3, keepdims=True))
        probs = jnp.exp(scores - log_total)
        dprobs = jnp.einsum("qkgd,skd->kgqs", grads_float, complete_values)
        delta = jnp.sum(probs * dprobs, axis=3, keepdims=True)
        dscores = lax.optimization_barrier((probs * (dprobs - delta)).astype(jnp.bfloat16)).astype(jnp.float32)
        probs_low = lax.optimization_barrier(probs.astype(jnp.bfloat16)).astype(jnp.float32)
        query_grad = jnp.einsum("kgqs,skd->qkgd", dscores, complete_keys) * score_scale
        key_accumulator = key_accumulator + jnp.einsum("kgqs,qkgd->skd", dscores, query_float) * score_scale
        value_accumulator = value_accumulator + jnp.einsum("kgqs,qkgd->skd", probs_low, grads_float)
        return (key_accumulator, value_accumulator), query_grad

    zero_start = jnp.zeros((SEQUENCE_LENGTH, KEY_VALUE_HEADS, HEAD_SIZE), jnp.float32)
    (key_accumulator, value_accumulator), query_grads = lax.scan(advance, (zero_start, zero_start), (blocked_queries, gradient_blocks, pos_blocks))
    query_gradient = query_grads.reshape(SEQUENCE_LENGTH, QUERY_HEADS * HEAD_SIZE)
    return query_gradient, key_accumulator.reshape(SEQUENCE_LENGTH, KEY_VALUE_HEADS * HEAD_SIZE), value_accumulator.reshape(SEQUENCE_LENGTH, KEY_VALUE_HEADS * HEAD_SIZE)
```

```python
import jax
import jax.numpy as jnp
from jax import lax
from jax.experimental import pallas as pl
from jax.experimental.pallas import tpu as pltpu
from jax.sharding import Mesh, PartitionSpec as P

HEAD = 128
HEADS = 6
SPAN = 64
SPANS = 128
ROWS = HEADS * SPAN
BLOCK = 256
PER_BLOCK = BLOCK // SPAN
STEPS = SPANS // PER_BLOCK + 1
SEQ = SPANS * SPAN
LOG2E = 1.4426950408889634
SCALE = HEAD ** -0.5
NZ, NX, NC, NY = 8, 4, 2, 4


def attention_kernel(*refs):
    meta, pair, q_ref, g_ref = refs[:4]
    chunks = refs[4:20]
    dq_ref, out_ref = refs[20:22]
    (kv, e_s, d_s, acc, stage, q_n, g_n, q_t, g_t, m_s, l_s, w_s, fac, dq_t,
     in_sem, out_sem) = refs[22:]
    z, x, c = meta[0], meta[1], meta[2]
    mine = pair[(z * NX + x) * NC + c]

    copies = []
    for a in range(16):
        dz, dc = a // 2, a % 2
        for dx in range(NX):
            who = (((z + NZ - dz) % NZ) * NX + (x + NX - dx) % NX) * NC + (c + dc) % NC
            p = pair[who]
            for half, span in ((0, p), (1, SPANS - 1 - p)):
                n = (a * NX + dx) * 2 + half
                copy = pltpu.make_async_copy(
                    chunks[a].at[dx, pl.ds(half * SPAN, SPAN), :],
                    kv.at[pl.ds(pl.multiple_of(span * SPAN, SPAN), SPAN), :],
                    in_sem.at[n],
                )
                copy.start()
                copies.append(copy)

    acc[...] = jnp.zeros_like(acc)
    dq_t[...] = jnp.zeros_like(dq_t)
    for s in range(2):
        for h in range(HEADS):
            rows = pl.ds(s * SPAN, SPAN)
            cols = pl.ds(h * HEAD, HEAD)
            q_n[s, pl.ds(h * SPAN, SPAN), :] = q_ref[rows, cols]
            g_n[s, pl.ds(h * SPAN, SPAN), :] = g_ref[rows, cols]
        q_t[s] = q_n[s].T
        g_t[s] = g_n[s].T
    for copy in copies:
        copy.wait()

    spans = (mine, SPANS - 1 - mine)
    n_low = spans[0] // PER_BLOCK + 1
    n_high = spans[1] // PER_BLOCK + 1

    def first(t, s, j, masked):
        keys = kv[pl.ds(pl.multiple_of(j * BLOCK, BLOCK), BLOCK), 0:HEAD]
        vals = kv[pl.ds(pl.multiple_of(j * BLOCK, BLOCK), BLOCK), HEAD:2 * HEAD]
        sc = jnp.dot(keys, q_t[s], preferred_element_type=jnp.float32)
        dp = jnp.dot(vals, g_t[s], preferred_element_type=jnp.float32)
        if masked:
            kp = j * BLOCK + lax.broadcasted_iota(jnp.int32, sc.shape, 0)
            qp = spans[s] * SPAN + lax.broadcasted_iota(jnp.int32, sc.shape, 1) % SPAN
            sc = jnp.where(kp <= qp, sc, -jnp.inf)
        m = jnp.max(sc, axis=0, keepdims=True)
        e = jnp.exp2((sc - m) * (SCALE * LOG2E))
        e_s[t] = e
        d_s[t] = dp
        m_s[t] = jnp.broadcast_to(m, (8, ROWS))
        l_s[t] = jnp.broadcast_to(jnp.sum(e, axis=0, keepdims=True), (8, ROWS))
        w_s[t] = jnp.broadcast_to(jnp.sum(e * dp, axis=0, keepdims=True), (8, ROWS))

    first(0, 0, n_low - 1, True)
    first(1, 1, n_high - 1, True)

    def place(t):
        low = t < n_low - 1
        s = jnp.where(low, 0, 1)
        j = jnp.where(low, t, t - (n_low - 1))
        return s, j

    def first_body(t, carry):
        s, j = place(t)
        first(t + 2, s, j, False)
        return carry

    lax.fori_loop(0, STEPS - 2, first_body, 0)

    def step_is_low(t):
        return jnp.logical_or(t == 0, jnp.logical_and(t >= 2, t - 2 < n_low - 1))

    neg = jnp.full((8, ROWS), -jnp.inf, jnp.float32)

    def max_body(t, carry):
        lo, hi = carry
        low = step_is_low(t)
        m = m_s[t]
        return (jnp.maximum(lo, jnp.where(low, m, neg)), jnp.maximum(hi, jnp.where(low, neg, m)))

    top = lax.fori_loop(0, STEPS, max_body, (neg, neg))
    zero = jnp.zeros((8, ROWS), jnp.float32)

    def sum_body(t, carry):
        l0, w0, l1, w1 = carry
        low = step_is_low(t)
        f = jnp.exp2((m_s[t] - jnp.where(low, top[0], top[1])) * (SCALE * LOG2E))
        fac[t] = f
        l = l_s[t] * f
        w = w_s[t] * f
        return (
            l0 + jnp.where(low, l, zero),
            w0 + jnp.where(low, w, zero),
            l1 + jnp.where(low, zero, l),
            w1 + jnp.where(low, zero, w),
        )

    l0, w0, l1, w1 = lax.fori_loop(0, STEPS, sum_body, (zero, zero, zero, zero))
    inv = (1.0 / l0, 1.0 / l1)
    delta = (w0 / l0, w1 / l1)

    def second(t, s, j):
        low = s == 0
        f = (fac[t] * jnp.where(low, inv[0], inv[1]))[0:1, :]
        dl = jnp.where(low, delta[0], delta[1])[0:1, :]
        p = e_s[t] * f
        ds = (p * (d_s[t] - dl)).astype(jnp.bfloat16)
        pb = p.astype(jnp.bfloat16)
        rows = pl.ds(pl.multiple_of(j * BLOCK, BLOCK), BLOCK)
        keys = kv[rows, 0:HEAD]
        acc[rows, 0:HEAD] += jnp.dot(ds, q_n[s], preferred_element_type=jnp.float32)
        acc[rows, HEAD:2 * HEAD] += jnp.dot(pb, g_n[s], preferred_element_type=jnp.float32)
        dq_t[s] += lax.dot_general(
            keys, ds, (((0,), (0,)), ((), ())), preferred_element_type=jnp.float32
        )

    second(0, 0, n_low - 1)
    second(1, 1, n_high - 1)

    def second_body(t, carry):
        s, j = place(t)
        second(t + 2, s, j)
        return carry

    lax.fori_loop(0, STEPS - 2, second_body, 0)

    def cast_body(j, carry):
        rows = pl.ds(pl.multiple_of(j * BLOCK, BLOCK), BLOCK)
        stage[rows, 0:HEAD] = (acc[rows, 0:HEAD] * SCALE).astype(jnp.bfloat16)
        stage[rows, HEAD:2 * HEAD] = acc[rows, HEAD:2 * HEAD].astype(jnp.bfloat16)
        return carry

    lax.fori_loop(0, SEQ // BLOCK, cast_body, 0)
    copies = []
    for dc in range(NC):
        for dx in range(NX):
            for zd in range(NZ):
                who = (zd * NX + (x + dx) % NX) * NC + (c + dc) % NC
                p = pair[who]
                for half, span in ((0, p), (1, SPANS - 1 - p)):
                    n = ((dc * NX + dx) * NZ + zd) * 2 + half
                    copy = pltpu.make_async_copy(
                        stage.at[pl.ds(pl.multiple_of(span * SPAN, SPAN), SPAN), :],
                        out_ref.at[dc, dx, zd, pl.ds(half * SPAN, SPAN), :],
                        out_sem.at[n],
                    )
                    copy.start()
                    copies.append(copy)
    for s in range(2):
        dq = dq_t[s].T * SCALE
        for h in range(HEADS):
            dq_ref[pl.ds(s * SPAN, SPAN), pl.ds(h * HEAD, HEAD)] = dq[h * SPAN:(h + 1) * SPAN, :]
    for copy in copies:
        copy.wait()


def attention(meta, pair_order, queries, head_grads, chunks):
    smem = pl.BlockSpec(memory_space=pltpu.SMEM)
    vmem = pl.BlockSpec(memory_space=pltpu.VMEM)
    hbm = pl.BlockSpec(memory_space=pl.ANY)
    return pl.pallas_call(
        attention_kernel,
        out_shape=(
            jax.ShapeDtypeStruct((2 * SPAN, HEADS * HEAD), jnp.float32),
            jax.ShapeDtypeStruct((NC, NX, NZ, 2 * SPAN, 2 * HEAD), jnp.bfloat16),
        ),
        in_specs=[smem, smem, vmem, vmem] + [hbm] * 16,
        out_specs=(vmem, hbm),
        scratch_shapes=[
            pltpu.VMEM((SEQ, 2 * HEAD), jnp.bfloat16),
            pltpu.VMEM((STEPS, BLOCK, ROWS), jnp.float32),
            pltpu.VMEM((STEPS, BLOCK, ROWS), jnp.float32),
            pltpu.VMEM((SEQ, 2 * HEAD), jnp.float32),
            pltpu.VMEM((SEQ, 2 * HEAD), jnp.bfloat16),
            pltpu.VMEM((2, ROWS, HEAD), jnp.bfloat16),
            pltpu.VMEM((2, ROWS, HEAD), jnp.bfloat16),
            pltpu.VMEM((2, HEAD, ROWS), jnp.bfloat16),
            pltpu.VMEM((2, HEAD, ROWS), jnp.bfloat16),
            pltpu.VMEM((STEPS, 8, ROWS), jnp.float32),
            pltpu.VMEM((STEPS, 8, ROWS), jnp.float32),
            pltpu.VMEM((STEPS, 8, ROWS), jnp.float32),
            pltpu.VMEM((STEPS, 8, ROWS), jnp.float32),
            pltpu.VMEM((2, HEAD, ROWS), jnp.float32),
            pltpu.SemaphoreType.DMA((128,)),
            pltpu.SemaphoreType.DMA((128,)),
        ],
        compiler_params=pltpu.CompilerParams(vmem_limit_bytes=56 * 1024 * 1024),
        cost_estimate=pl.CostEstimate(flops=9 * 10**9, bytes_accessed=10**7, transcendentals=0),
        name="attention",
    )(meta, pair_order, queries, head_grads, *chunks)


def shift(value, axis, distance):
    size = lax.axis_size(axis)
    return lax.ppermute(value, axis, [(i, (i + distance) % size) for i in range(size)])


def wide(value):
    return value.astype(jnp.float32)


def shards(queries, keys, values, out_grad, out_weight, pair_order):
    y = lax.axis_index("y")
    meta = jnp.stack([lax.axis_index("z"), lax.axis_index("x"), lax.axis_index("c")])
    meta = meta.astype(jnp.int32)

    parts = [out_grad] + [shift(out_grad, "y", k) for k in (1, 2, 3)]
    whole = jnp.zeros((2 * SPAN, out_grad.shape[1] * NY), out_grad.dtype)
    for k, part in enumerate(parts):
        whole = lax.dynamic_update_slice(
            whole, part, (0, ((y + NY - k) % NY) * out_grad.shape[1])
        )
    head_grads = lax.dot_general(
        whole, out_weight, (((1,), (1,)), ((), ())), preferred_element_type=jnp.float32
    ).astype(jnp.bfloat16)

    own = jnp.concatenate([keys, values], axis=1)
    line = jnp.stack([own] + [shift(own, "x", k) for k in (1, 2, 3)])
    ahead, behind = line, line
    by_z = {0: line}
    for k in (1, 2, 3):
        ahead = shift(ahead, "z", 1)
        behind = shift(behind, "z", -1)
        by_z[k], by_z[NZ - k] = ahead, behind
    by_z[4] = jnp.concatenate([shift(ahead[:2], "z", 1), shift(behind[2:], "z", -1)])
    chunks = []
    for k in range(NZ):
        chunks += [by_z[k], shift(by_z[k], "c", 1)]

    query_gradient, terms = attention(meta, pair_order, queries, head_grads, chunks)

    other = shift(terms[1], "c", 1)
    terms = (wide(terms[0]) + wide(other)).astype(jnp.bfloat16)
    total = wide(terms[0])
    for k in (1, 2, 3):
        total = total + wide(shift(terms[k], "x", k))
    total = lax.all_to_all(total.astype(jnp.bfloat16), "z", 0, 0, tiled=True)
    total = jnp.sum(wide(total), axis=0)
    return query_gradient, total[:, :HEAD], total[:, HEAD:]


def solution(mesh):
    split = Mesh(mesh.devices.reshape(NZ, NX, NC, NY), ("z", "x", "c", "y"))
    ctx = ("z", "x", "c")
    return jax.shard_map(
        shards,
        mesh=split,
        in_specs=(P(ctx, "y"), P(ctx, "y"), P(ctx, "y"), P(ctx, "y"), P("y", None), P()),
        out_specs=(P(ctx, "y"), P(ctx, "y"), P(ctx, "y")),
        check_vma=False,
    )
```

```python
import jax
import jax.numpy as jnp
from jax import lax
from jax.experimental import pallas as pl
from jax.experimental.pallas import tpu as pltpu
from jax.sharding import Mesh, PartitionSpec as P

HEAD = 128
HEADS = 6
SPAN = 64
SPANS = 128
ROWS = HEADS * SPAN
BLOCK = 256
PER_BLOCK = BLOCK // SPAN
LOG2E = 1.4426950408889634
SCALE = HEAD ** -0.5
NZ, NX, NC, NY = 8, 4, 2, 4
QSETS = 2 * NX
KEY_DEVICES = NZ * NC
KEY_SPANS = 2 * KEY_DEVICES
KEYS = KEY_SPANS * SPAN
MAX_STEPS = 48
T_RANK, T_SPAN, T_QSPAN, T_QSET, T_BLOCK, T_COUNT, T_X, T_C = (
    0, 16, 48, 64, 112, 160, 161, 162
)
TABLE = 192
SPREAD_FLOPS = 2 * 10**10
LOW = -1e30
PAIR_STEPS = 2


def table_kernel(pair, table):
    z, x, c = lax.axis_index("z"), lax.axis_index("x"), lax.axis_index("c")
    keys = [pair[((i // NC) * NX + x) * NC + i % NC] for i in range(KEY_DEVICES)]
    ranks = [jnp.int32(0)] * KEY_DEVICES
    for i in range(KEY_DEVICES):
        for j in range(i):
            less = (keys[j] < keys[i]).astype(jnp.int32)
            ranks[i] = ranks[i] + less
            ranks[j] = ranks[j] + (1 - less)
    for i in range(KEY_DEVICES):
        table[T_RANK + i] = ranks[i]
        table[T_SPAN + ranks[i]] = keys[i]
        table[T_SPAN + KEY_SPANS - 1 - ranks[i]] = SPANS - 1 - keys[i]
    table[T_X] = x
    table[T_C] = c
    end = jnp.int32(0)
    for u in range(QSETS):
        low = pair[(z * NX + u // 2) * NC + c]
        below = jnp.int32(0)
        same = jnp.int32(0)
        for key in keys:
            below = below + (key < low).astype(jnp.int32)
            same = same + (key == low).astype(jnp.int32)
        if u % 2 == 0:
            table[T_QSPAN + u] = low
            seen = below + same
        else:
            table[T_QSPAN + u] = SPANS - 1 - low
            seen = KEY_SPANS - below
        count = (seen + PER_BLOCK - 1) // PER_BLOCK

        def fill(j, carry, u=u, end=end):
            table[T_QSET + end + j] = u
            table[T_BLOCK + end + j] = j
            return carry

        lax.fori_loop(0, count, fill, 0)
        end = end + count
    table[T_COUNT] = end
    table[T_QSPAN + QSETS] = -SPANS
    table[T_QSET + end] = QSETS
    table[T_BLOCK + end] = 0


def tables(pair_order):
    return pl.pallas_call(
        table_kernel,
        out_shape=jax.ShapeDtypeStruct((TABLE,), jnp.int32),
        in_specs=[SMEM],
        out_specs=SMEM,
        cost_estimate=pl.CostEstimate(flops=10**6, bytes_accessed=10**3, transcendentals=0),
        name="tables",
    )(pair_order)


def masked_scores(table, keys, q_t, u, j):
    sc = jnp.dot(keys, q_t[u], preferred_element_type=jnp.float32)
    row = lax.broadcasted_iota(jnp.int32, (SPAN, ROWS), 0)
    col = lax.broadcasted_iota(jnp.int32, (SPAN, ROWS), 1) % SPAN
    ahead = row - col
    q_span = table[T_QSPAN + u]
    pieces = []
    for i in range(PER_BLOCK):
        room = (q_span - table[T_SPAN + j * PER_BLOCK + i]) * SPAN
        pieces.append(jnp.where(ahead <= room, sc[i * SPAN:(i + 1) * SPAN, :], -jnp.inf))
    return jnp.concatenate(pieces, axis=0)


def block_rows(j):
    return pl.ds(pl.multiple_of(j * BLOCK, BLOCK), BLOCK)


def forward_kernel(table, *refs):
    queries = refs[:NX]
    own, other, kv, q_n, q_t, stats, o_t, m_s = refs[NX:]
    x = table[T_X]
    for i in range(KEY_DEVICES):
        dc, z = i // NZ, i % NZ
        chunk = (own, other)[dc]
        rank = table[T_RANK + z * NC + (table[T_C] + dc) % NC]
        for half, slot in ((0, rank), (1, KEY_SPANS - 1 - rank)):
            kv[pl.ds(pl.multiple_of(slot * SPAN, SPAN), SPAN), :] = (
                chunk[z, pl.ds(half * SPAN, SPAN), :]
            )
    for dx in range(NX):
        base = ((x + NX - dx) % NX) * 2
        for s in range(2):
            for h in range(HEADS):
                q_n[base + s, pl.ds(h * SPAN, SPAN), :] = (
                    queries[dx][pl.ds(s * SPAN, SPAN), pl.ds(h * HEAD, HEAD)]
                )
            q_t[base + s] = q_n[base + s].T
    q_t[QSETS] = jnp.zeros((HEAD, ROWS), jnp.bfloat16)
    o_t[...] = jnp.zeros_like(o_t)
    stats[1] = jnp.zeros((QSETS + 1, 8, ROWS), jnp.float32)
    m_s[...] = jnp.full_like(m_s, LOW)

    def body(i, carry):
        us = [table[T_QSET + i * PAIR_STEPS + k] for k in range(PAIR_STEPS)]
        js = [table[T_BLOCK + i * PAIR_STEPS + k] for k in range(PAIR_STEPS)]
        scs = [masked_scores(table, kv[block_rows(j), 0:HEAD], q_t, u, j) for u, j in zip(us, js)]
        tops = [jnp.max(sc, axis=0, keepdims=True) for sc in scs]
        for u, j, sc, top in zip(us, js, scs, tops):
            old = m_s[u]
            new = jnp.maximum(old, top)
            f = jnp.exp2((old - new) * (SCALE * LOG2E))
            e = jnp.exp2((sc - new[0:1, :]) * (SCALE * LOG2E))
            m_s[u] = new
            stats[1, u] = stats[1, u] * f + jnp.sum(e, axis=0, keepdims=True)
            o_t[u] = o_t[u] * f[0:1, :] + lax.dot_general(
                kv[block_rows(j), HEAD:2 * HEAD], e.astype(jnp.bfloat16),
                (((0,), (0,)), ((), ())), preferred_element_type=jnp.float32,
            )
        return carry

    lax.fori_loop(0, (table[T_COUNT] + PAIR_STEPS - 1) // PAIR_STEPS, body, 0)
    stats[0] = m_s[...]


def weight_kernel(table, *refs):
    grads = refs[:NX]
    stats, o_t = refs[NX:NX + 2]
    g_n, g_t, stats_out = refs[NX + 2:]
    x = table[T_X]
    for dx in range(NX):
        base = ((x + NX - dx) % NX) * 2
        for s in range(2):
            u = base + s
            for h in range(HEADS):
                g_n[u, pl.ds(h * SPAN, SPAN), :] = (
                    grads[dx][pl.ds(s * SPAN, SPAN), pl.ds(h * HEAD, HEAD)]
                )
            turned = g_n[u].T
            g_t[u] = turned
            w = jnp.sum(turned.astype(jnp.float32) * o_t[u], axis=0, keepdims=True)
            stats_out[2, pl.ds(u, 1), :] = w
            stats_out[0, pl.ds(u, 1), :] = stats[0, u, 0:1, :]
            stats_out[1, pl.ds(u, 1), :] = stats[1, u, 0:1, :]
    g_n[QSETS] = jnp.zeros((ROWS, HEAD), jnp.bfloat16)
    g_t[QSETS] = jnp.zeros((HEAD, ROWS), jnp.bfloat16)


def backward_kernel(table, *refs):
    stats = refs[:NX]
    kv, q_n, q_t, g_n, g_t, own_ref, part_ref, out_ref = refs[NX:NX + 8]
    acc, dq_t, lse_s, delta_s = refs[NX + 8:]
    x = table[T_X]
    top = stats[0][0]
    for r in stats[1:]:
        top = jnp.maximum(top, r[0])
    total = jnp.zeros((QSETS, ROWS), jnp.float32)
    weight = jnp.zeros((QSETS, ROWS), jnp.float32)
    for r in stats:
        f = jnp.exp2((r[0] - top) * (SCALE * LOG2E))
        total = total + r[1] * f
        weight = weight + r[2] * f
    lse = top * (SCALE * LOG2E) + jnp.log2(total)
    delta = weight / total
    for u in range(QSETS):
        lse_s[u] = jnp.broadcast_to(lse[u:u + 1, :], (8, ROWS))
        delta_s[u] = jnp.broadcast_to(delta[u:u + 1, :], (8, ROWS))
    lse_s[QSETS] = jnp.zeros((8, ROWS), jnp.float32)
    delta_s[QSETS] = jnp.zeros((8, ROWS), jnp.float32)
    acc[...] = jnp.zeros_like(acc)
    dq_t[...] = jnp.zeros_like(dq_t)

    def body(i, carry):
        us = [table[T_QSET + i * PAIR_STEPS + k] for k in range(PAIR_STEPS)]
        js = [table[T_BLOCK + i * PAIR_STEPS + k] for k in range(PAIR_STEPS)]
        scs = [masked_scores(table, kv[block_rows(j), 0:HEAD], q_t, u, j) for u, j in zip(us, js)]
        dps = [
            jnp.dot(kv[block_rows(j), HEAD:2 * HEAD], g_t[u], preferred_element_type=jnp.float32)
            for u, j in zip(us, js)
        ]
        for u, j, sc, dp in zip(us, js, scs, dps):
            p = jnp.exp2(sc * (SCALE * LOG2E) - lse_s[u][0:1, :])
            ds = (p * (dp - delta_s[u][0:1, :])).astype(jnp.bfloat16)
            rows = block_rows(j)
            acc[rows, HEAD:2 * HEAD] += jnp.dot(
                p.astype(jnp.bfloat16), g_n[u], preferred_element_type=jnp.float32
            )
            acc[rows, 0:HEAD] += jnp.dot(ds, q_n[u], preferred_element_type=jnp.float32)
            dq_t[u] += lax.dot_general(
                kv[rows, 0:HEAD], ds, (((0,), (0,)), ((), ())), preferred_element_type=jnp.float32
            )
        return carry

    lax.fori_loop(0, (table[T_COUNT] + PAIR_STEPS - 1) // PAIR_STEPS, body, 0)

    for i in range(KEY_DEVICES):
        rank = table[T_RANK + i]
        place = ((i + table[T_C]) % NC) * NZ + i // NC
        for half, slot in ((0, rank), (1, KEY_SPANS - 1 - rank)):
            rows = pl.ds(pl.multiple_of(slot * SPAN, SPAN), SPAN)
            out_ref[place, pl.ds(half * SPAN, SPAN), 0:HEAD] = (acc[rows, 0:HEAD] * SCALE).astype(jnp.bfloat16)
            out_ref[place, pl.ds(half * SPAN, SPAN), HEAD:2 * HEAD] = (
                acc[rows, HEAD:2 * HEAD].astype(jnp.bfloat16)
            )
    for dx in range(NX):
        base = ((x + dx) % NX) * 2
        for s in range(2):
            dq = dq_t[base + s].T * SCALE
            for h in range(HEADS):
                piece = dq[h * SPAN:(h + 1) * SPAN, :]
                rows, cols = pl.ds(s * SPAN, SPAN), pl.ds(h * HEAD, HEAD)
                if dx == 0:
                    own_ref[rows, cols] = piece
                else:
                    part_ref[dx - 1, rows, cols] = piece.astype(jnp.bfloat16)


def part_columns(k, columns):
    owner = (lax.axis_index("y") + NY - k) % NY
    return pl.ds(pl.multiple_of(owner * columns, columns), columns)


def weight_product(weight, part):
    return lax.dot_general(
        weight, part[...], (((1,), (1,)), ((), ())), preferred_element_type=jnp.float32
    )


def project_own_kernel(own, w_ref, unread, sum_ref, rest_ref):
    columns = own.shape[1]
    sum_ref[...] = weight_product(w_ref[:, part_columns(0, columns)], own)
    for k in range(1, NY):
        rest_ref[k - 1] = w_ref[:, part_columns(k, columns)]


def project_near_kernel(one, three, rest, sum_ref, out_ref):
    out_ref[...] = (
        sum_ref[...] + weight_product(rest[0], one) + weight_product(rest[2], three)
    )


def project_far_kernel(part, rest, sum_ref, *refs):
    out_ref = refs[-1]
    out_ref[...] = (sum_ref[...] + weight_product(rest[1], part)).T.astype(jnp.bfloat16)


def project_call(body, name, outs, flops, operands, unread=()):
    specs = [VMEM] * len(operands) + [pl.BlockSpec(memory_space=pl.ANY)] * len(unread)
    return pl.pallas_call(
        body,
        out_shape=tuple(jax.ShapeDtypeStruct(s, d) for s, d in outs),
        in_specs=specs,
        out_specs=tuple(VMEM for _ in outs),
        compiler_params=pltpu.CompilerParams(vmem_limit_bytes=24 * 1024 * 1024),
        cost_estimate=pl.CostEstimate(flops=flops, bytes_accessed=10**6, transcendentals=0),
        name=name,
    )(*operands, *unread)


SMEM = pl.BlockSpec(memory_space=pltpu.SMEM)
VMEM = pl.BlockSpec(memory_space=pltpu.VMEM)


def kernel_call(body, name, outs, scratch, flops, *operands):
    return pl.pallas_call(
        body,
        out_shape=tuple(jax.ShapeDtypeStruct(s, d) for s, d in outs),
        in_specs=[SMEM] + [VMEM] * (len(operands) - 1),
        out_specs=tuple(VMEM for _ in outs),
        scratch_shapes=[pltpu.VMEM(s, d) for s, d in scratch],
        compiler_params=pltpu.CompilerParams(vmem_limit_bytes=40 * 1024 * 1024),
        cost_estimate=pl.CostEstimate(flops=flops, bytes_accessed=10**6, transcendentals=0),
        name=name,
    )(*operands)


def spread_kernel(keys, values, copies):
    for k in range(NZ):
        copies[k, :, 0:HEAD] = keys[...]
        copies[k, :, HEAD:2 * HEAD] = values[...]


def after_kernel(*refs):
    pass


def after(value, *others):
    anywhere = pl.BlockSpec(memory_space=pl.ANY)
    return pl.pallas_call(
        after_kernel,
        out_shape=jax.ShapeDtypeStruct(value.shape, value.dtype),
        in_specs=[anywhere] * (1 + len(others)),
        out_specs=anywhere,
        input_output_aliases={0: 0},
        name="after",
    )(value, *others)


def shift(value, axis, distance):
    size = lax.axis_size(axis)
    return lax.ppermute(value, axis, [(i, (i + distance) % size) for i in range(size)])


def wide(value):
    return value.astype(jnp.float32)


def shards(queries, keys, values, out_grad, out_weight, pair_order):
    table = tables(pair_order)
    bf16, f32 = jnp.bfloat16, jnp.float32

    parts = {k: shift(out_grad, "y", k) for k in (1, 3, 2)}
    copies = pl.pallas_call(
        spread_kernel,
        out_shape=jax.ShapeDtypeStruct((NZ, 2 * SPAN, 2 * HEAD), bf16),
        in_specs=[VMEM, VMEM],
        out_specs=VMEM,
        cost_estimate=pl.CostEstimate(flops=SPREAD_FLOPS, bytes_accessed=10**6, transcendentals=0),
        name="spread",
    )(keys, values)
    rows, columns = out_grad.shape
    heads = out_weight.shape[0]
    summed, rest = project_call(
        project_own_kernel, "project_own", [((heads, rows), f32), ((NY - 1, heads, columns), bf16)],
        3 * 10**8, [out_grad, out_weight], [copies],
    )
    all_queries = [queries] + [shift(queries, "x", k) for k in (1, 2, 3)]
    (summed,) = project_call(
        project_near_kernel, "project_near", [((heads, rows), f32)], 6 * 10**8,
        [parts[1], parts[3], rest, summed],
    )
    (head_grads,) = project_call(
        project_far_kernel, "project_far", [((rows, heads), bf16)], 3 * 10**8,
        [parts[2], rest, summed], [table],
    )

    along_z = lax.all_to_all(copies, "z", 0, 0, tiled=True)
    along_z = after(along_z, head_grads, all_queries[1], all_queries[3])
    chunks = [along_z, shift(along_z, "c", 1)]

    kv, q_n, q_t, stats, o_t = kernel_call(
        forward_kernel, "forward",
        [((KEYS, 2 * HEAD), bf16), ((QSETS + 1, ROWS, HEAD), bf16), ((QSETS + 1, HEAD, ROWS), bf16),
         ((2, QSETS + 1, 8, ROWS), f32), ((QSETS + 1, HEAD, ROWS), f32)],
        [((QSETS + 1, 8, ROWS), f32)],
        4 * 10**9, table, *all_queries, *chunks,
    )
    all_grads = [head_grads] + [shift(head_grads, "x", k) for k in (1, 2, 3)]
    g_n, g_t, stats = kernel_call(
        weight_kernel, "weights",
        [((QSETS + 1, ROWS, HEAD), bf16), ((QSETS + 1, HEAD, ROWS), bf16), ((3, QSETS, ROWS), f32)],
        [], 10**7, table, *all_grads, stats, o_t,
    )
    all_stats = [stats] + [shift(stats, "x", k) for k in (1, 2, 3)]
    query_own, query_parts, terms = kernel_call(
        backward_kernel, "backward",
        [((2 * SPAN, HEADS * HEAD), f32), ((NX - 1, 2 * SPAN, HEADS * HEAD), bf16),
         ((KEY_DEVICES, 2 * SPAN, 2 * HEAD), bf16)],
        [((KEYS, 2 * HEAD), f32), ((QSETS + 1, HEAD, ROWS), f32), ((QSETS + 1, 8, ROWS), f32),
         ((QSETS + 1, 8, ROWS), f32)],
        8 * 10**9, table, *all_stats, kv, q_n, q_t, g_n, g_t,
    )
    query_gradient = query_own
    for k in (1, 2, 3):
        query_gradient = query_gradient + wide(shift(query_parts[k - 1], "x", k))

    terms = terms.reshape(NC, NZ, 2 * SPAN, 2 * HEAD)
    total = wide(terms[0]) + wide(shift(terms[1], "c", 1))
    total = lax.all_to_all(total.astype(bf16), "z", 0, 0, tiled=True)
    total = jnp.sum(wide(total), axis=0)
    return query_gradient, total[:, :HEAD], total[:, HEAD:]


def solution(mesh):
    split = Mesh(mesh.devices.reshape(NZ, NX, NC, NY), ("z", "x", "c", "y"))
    ctx = ("z", "x", "c")
    return jax.shard_map(
        shards,
        mesh=split,
        in_specs=(P(ctx, "y"), P(ctx, "y"), P(ctx, "y"), P(ctx, "y"), P("y", None), P()),
        out_specs=(P(ctx, "y"), P(ctx, "y"), P(ctx, "y")),
        check_vma=False,
    )
```

```python
import jax
import jax.numpy as jnp
from jax import lax
from jax.experimental import pallas as pl
from jax.experimental.pallas import tpu as pltpu
from jax.sharding import Mesh, PartitionSpec as P

HEAD = 128
HEADS = 6
SPAN = 64
SPANS = 128
ROWS = HEADS * SPAN
BLOCK = 256
PER_BLOCK = BLOCK // SPAN
LOG2E = 1.4426950408889634
SCALE = HEAD ** -0.5
NZ, NX, NC, NY = 8, 4, 2, 4
QSETS = 2 * NX
KEY_DEVICES = NZ * NC
KEY_SPANS = 2 * KEY_DEVICES
KEYS = KEY_SPANS * SPAN
MAX_STEPS = 48
T_RANK, T_SPAN, T_QSPAN, T_QSET, T_BLOCK, T_COUNT, T_X, T_C, T_FULL = (
    0, 16, 48, 64, 112, 160, 161, 162, 163
)
TABLE = 192
SPREAD_FLOPS = 2 * 10**10
LOW = -1e30
PAIR_STEPS = 4


def table_kernel(pair, table):
    z, x, c = lax.axis_index("z"), lax.axis_index("x"), lax.axis_index("c")
    keys = [pair[((i // NC) * NX + x) * NC + i % NC] for i in range(KEY_DEVICES)]
    ranks = [jnp.int32(0)] * KEY_DEVICES
    for i in range(KEY_DEVICES):
        for j in range(i):
            less = (keys[j] < keys[i]).astype(jnp.int32)
            ranks[i] = ranks[i] + less
            ranks[j] = ranks[j] + (1 - less)
    for i in range(KEY_DEVICES):
        table[T_RANK + i] = ranks[i]
        table[T_SPAN + ranks[i]] = keys[i]
        table[T_SPAN + KEY_SPANS - 1 - ranks[i]] = SPANS - 1 - keys[i]
    table[T_X] = x
    table[T_C] = c
    end = jnp.int32(0)
    lasts = []
    for u in range(QSETS):
        low = pair[(z * NX + u // 2) * NC + c]
        below = jnp.int32(0)
        same = jnp.int32(0)
        for key in keys:
            below = below + (key < low).astype(jnp.int32)
            same = same + (key == low).astype(jnp.int32)
        if u % 2 == 0:
            table[T_QSPAN + u] = low
            seen = below + same
        else:
            table[T_QSPAN + u] = SPANS - 1 - low
            seen = KEY_SPANS - below
        last = (seen + PER_BLOCK - 1) // PER_BLOCK - 1
        lasts.append(last)

        def fill(j, carry, u=u, end=end):
            table[T_QSET + end + j] = u
            table[T_BLOCK + end + j] = j
            return carry

        lax.fori_loop(0, last, fill, 0)
        end = end + jnp.maximum(last, 0)
    table[T_FULL] = end // PAIR_STEPS * PAIR_STEPS
    for u in range(QSETS):
        none = lasts[u] < 0
        table[T_QSET + end + u] = jnp.where(none, QSETS, u)
        table[T_BLOCK + end + u] = jnp.maximum(lasts[u], 0)
    table[T_COUNT] = end + QSETS
    table[T_QSPAN + QSETS] = -SPANS
    for k in range(PAIR_STEPS - 1):
        table[T_QSET + end + QSETS + k] = QSETS
        table[T_BLOCK + end + QSETS + k] = 0


def tables(pair_order):
    return pl.pallas_call(
        table_kernel,
        out_shape=jax.ShapeDtypeStruct((TABLE,), jnp.int32),
        in_specs=[SMEM],
        out_specs=SMEM,
        cost_estimate=pl.CostEstimate(flops=10**6, bytes_accessed=10**3, transcendentals=0),
        name="tables",
    )(pair_order)


def masked_scores(table, keys, q_t, u, j, masked):
    sc = jnp.dot(keys, q_t[u], preferred_element_type=jnp.float32)
    if not masked:
        return sc
    row = lax.broadcasted_iota(jnp.int32, (SPAN, ROWS), 0)
    col = lax.broadcasted_iota(jnp.int32, (SPAN, ROWS), 1) % SPAN
    ahead = row - col
    q_span = table[T_QSPAN + u]
    pieces = []
    for i in range(PER_BLOCK):
        room = (q_span - table[T_SPAN + j * PER_BLOCK + i]) * SPAN
        pieces.append(jnp.where(ahead <= room, sc[i * SPAN:(i + 1) * SPAN, :], -jnp.inf))
    return jnp.concatenate(pieces, axis=0)


def step_loops(table, body):
    full = table[T_FULL] // PAIR_STEPS
    end = (table[T_COUNT] + PAIR_STEPS - 1) // PAIR_STEPS
    lax.fori_loop(0, full, lambda i, carry: body(i, carry, False), 0)
    lax.fori_loop(full, end, lambda i, carry: body(i, carry, True), 0)


def block_rows(j):
    return pl.ds(pl.multiple_of(j * BLOCK, BLOCK), BLOCK)


def forward_kernel(table, *refs):
    queries = refs[:NX]
    own, other, kv, q_n, q_t, stats, o_t, m_s = refs[NX:]
    x = table[T_X]
    for i in range(KEY_DEVICES):
        dc, z = i // NZ, i % NZ
        chunk = (own, other)[dc]
        rank = table[T_RANK + z * NC + (table[T_C] + dc) % NC]
        for half, slot in ((0, rank), (1, KEY_SPANS - 1 - rank)):
            kv[pl.ds(pl.multiple_of(slot * SPAN, SPAN), SPAN), :] = (
                chunk[z, pl.ds(half * SPAN, SPAN), :]
            )
    for dx in range(NX):
        base = ((x + NX - dx) % NX) * 2
        for s in range(2):
            for h in range(HEADS):
                q_n[base + s, pl.ds(h * SPAN, SPAN), :] = (
                    queries[dx][pl.ds(s * SPAN, SPAN), pl.ds(h * HEAD, HEAD)]
                )
            q_t[base + s] = q_n[base + s].T
    q_t[QSETS] = jnp.zeros((HEAD, ROWS), jnp.bfloat16)
    o_t[...] = jnp.zeros_like(o_t)
    stats[1] = jnp.zeros((QSETS + 1, 8, ROWS), jnp.float32)
    m_s[...] = jnp.full_like(m_s, LOW)

    def body(i, carry, masked):
        us = [table[T_QSET + i * PAIR_STEPS + k] for k in range(PAIR_STEPS)]
        js = [table[T_BLOCK + i * PAIR_STEPS + k] for k in range(PAIR_STEPS)]
        scs = [masked_scores(table, kv[block_rows(j), 0:HEAD], q_t, u, j, masked) for u, j in zip(us, js)]
        tops = [jnp.max(sc, axis=0, keepdims=True) for sc in scs]
        for u, j, sc, top in zip(us, js, scs, tops):
            old = m_s[u]
            new = jnp.maximum(old, top)
            f = jnp.exp2((old - new) * (SCALE * LOG2E))
            e = jnp.exp2((sc - new[0:1, :]) * (SCALE * LOG2E))
            m_s[u] = new
            stats[1, u] = stats[1, u] * f + jnp.sum(e, axis=0, keepdims=True)
            o_t[u] = o_t[u] * f[0:1, :] + lax.dot_general(
                kv[block_rows(j), HEAD:2 * HEAD], e.astype(jnp.bfloat16),
                (((0,), (0,)), ((), ())), preferred_element_type=jnp.float32,
            )
        return carry

    step_loops(table, body)
    stats[0] = m_s[...]


def weight_kernel(table, *refs):
    grads = refs[:NX]
    stats, o_t = refs[NX:NX + 2]
    g_n, g_t, stats_out = refs[NX + 2:]
    x = table[T_X]
    for dx in range(NX):
        base = ((x + NX - dx) % NX) * 2
        for s in range(2):
            u = base + s
            for h in range(HEADS):
                g_n[u, pl.ds(h * SPAN, SPAN), :] = (
                    grads[dx][pl.ds(s * SPAN, SPAN), pl.ds(h * HEAD, HEAD)]
                )
            turned = g_n[u].T
            g_t[u] = turned
            w = jnp.sum(turned.astype(jnp.float32) * o_t[u], axis=0, keepdims=True)
            stats_out[2, pl.ds(u, 1), :] = w
            stats_out[0, pl.ds(u, 1), :] = stats[0, u, 0:1, :]
            stats_out[1, pl.ds(u, 1), :] = stats[1, u, 0:1, :]
    g_n[QSETS] = jnp.zeros((ROWS, HEAD), jnp.bfloat16)
    g_t[QSETS] = jnp.zeros((HEAD, ROWS), jnp.bfloat16)


def backward_kernel(table, *refs):
    stats = refs[:NX]
    kv, q_n, q_t, g_n, g_t, own_ref, part_ref, out_ref = refs[NX:NX + 8]
    acc, dq_t, lse_s, delta_s = refs[NX + 8:]
    x = table[T_X]
    top = stats[0][0]
    for r in stats[1:]:
        top = jnp.maximum(top, r[0])
    total = jnp.zeros((QSETS, ROWS), jnp.float32)
    weight = jnp.zeros((QSETS, ROWS), jnp.float32)
    for r in stats:
        f = jnp.exp2((r[0] - top) * (SCALE * LOG2E))
        total = total + r[1] * f
        weight = weight + r[2] * f
    lse = top * (SCALE * LOG2E) + jnp.log2(total)
    delta = weight / total
    for u in range(QSETS):
        lse_s[u] = jnp.broadcast_to(lse[u:u + 1, :], (8, ROWS))
        delta_s[u] = jnp.broadcast_to(delta[u:u + 1, :], (8, ROWS))
    lse_s[QSETS] = jnp.zeros((8, ROWS), jnp.float32)
    delta_s[QSETS] = jnp.zeros((8, ROWS), jnp.float32)
    acc[...] = jnp.zeros_like(acc)
    dq_t[...] = jnp.zeros_like(dq_t)

    def body(i, carry, masked):
        us = [table[T_QSET + i * PAIR_STEPS + k] for k in range(PAIR_STEPS)]
        js = [table[T_BLOCK + i * PAIR_STEPS + k] for k in range(PAIR_STEPS)]
        scs = [masked_scores(table, kv[block_rows(j), 0:HEAD], q_t, u, j, masked) for u, j in zip(us, js)]
        dps = [
            jnp.dot(kv[block_rows(j), HEAD:2 * HEAD], g_t[u], preferred_element_type=jnp.float32)
            for u, j in zip(us, js)
        ]
        for u, j, sc, dp in zip(us, js, scs, dps):
            p = jnp.exp2(sc * (SCALE * LOG2E) - lse_s[u][0:1, :])
            ds = (p * (dp - delta_s[u][0:1, :])).astype(jnp.bfloat16)
            rows = block_rows(j)
            acc[rows, HEAD:2 * HEAD] += jnp.dot(
                p.astype(jnp.bfloat16), g_n[u], preferred_element_type=jnp.float32
            )
            acc[rows, 0:HEAD] += jnp.dot(ds, q_n[u], preferred_element_type=jnp.float32)
            dq_t[u] += lax.dot_general(
                kv[rows, 0:HEAD], ds, (((0,), (0,)), ((), ())), preferred_element_type=jnp.float32
            )
        return carry

    step_loops(table, body)

    for i in range(KEY_DEVICES):
        rank = table[T_RANK + i]
        place = ((i + table[T_C]) % NC) * NZ + i // NC
        for half, slot in ((0, rank), (1, KEY_SPANS - 1 - rank)):
            rows = pl.ds(pl.multiple_of(slot * SPAN, SPAN), SPAN)
            out_ref[place, pl.ds(half * SPAN, SPAN), 0:HEAD] = (acc[rows, 0:HEAD] * SCALE).astype(jnp.bfloat16)
            out_ref[place, pl.ds(half * SPAN, SPAN), HEAD:2 * HEAD] = (
                acc[rows, HEAD:2 * HEAD].astype(jnp.bfloat16)
            )
    for dx in range(NX):
        base = ((x + dx) % NX) * 2
        for s in range(2):
            dq = dq_t[base + s].T * SCALE
            for h in range(HEADS):
                piece = dq[h * SPAN:(h + 1) * SPAN, :]
                rows, cols = pl.ds(s * SPAN, SPAN), pl.ds(h * HEAD, HEAD)
                if dx == 0:
                    own_ref[rows, cols] = piece
                else:
                    part_ref[dx - 1, rows, cols] = piece.astype(jnp.bfloat16)


def part_columns(k, columns):
    owner = (lax.axis_index("y") + NY - k) % NY
    return pl.ds(pl.multiple_of(owner * columns, columns), columns)


def weight_product(weight, part):
    return lax.dot_general(
        weight, part[...], (((1,), (1,)), ((), ())), preferred_element_type=jnp.float32
    )


def project_own_kernel(own, w_ref, unread, sum_ref, rest_ref):
    columns = own.shape[1]
    sum_ref[...] = weight_product(w_ref[:, part_columns(0, columns)], own)
    for k in range(1, NY):
        rest_ref[k - 1] = w_ref[:, part_columns(k, columns)]


def project_near_kernel(one, three, rest, sum_ref, out_ref):
    out_ref[...] = (
        sum_ref[...] + weight_product(rest[0], one) + weight_product(rest[2], three)
    )


def project_far_kernel(part, rest, sum_ref, *refs):
    out_ref = refs[-1]
    out_ref[...] = (sum_ref[...] + weight_product(rest[1], part)).T.astype(jnp.bfloat16)


def project_call(body, name, outs, flops, operands, unread=()):
    specs = [VMEM] * len(operands) + [pl.BlockSpec(memory_space=pl.ANY)] * len(unread)
    return pl.pallas_call(
        body,
        out_shape=tuple(jax.ShapeDtypeStruct(s, d) for s, d in outs),
        in_specs=specs,
        out_specs=tuple(VMEM for _ in outs),
        compiler_params=pltpu.CompilerParams(vmem_limit_bytes=24 * 1024 * 1024),
        cost_estimate=pl.CostEstimate(flops=flops, bytes_accessed=10**6, transcendentals=0),
        name=name,
    )(*operands, *unread)


SMEM = pl.BlockSpec(memory_space=pltpu.SMEM)
VMEM = pl.BlockSpec(memory_space=pltpu.VMEM)


def kernel_call(body, name, outs, scratch, flops, *operands):
    return pl.pallas_call(
        body,
        out_shape=tuple(jax.ShapeDtypeStruct(s, d) for s, d in outs),
        in_specs=[SMEM] + [VMEM] * (len(operands) - 1),
        out_specs=tuple(VMEM for _ in outs),
        scratch_shapes=[pltpu.VMEM(s, d) for s, d in scratch],
        compiler_params=pltpu.CompilerParams(vmem_limit_bytes=40 * 1024 * 1024),
        cost_estimate=pl.CostEstimate(flops=flops, bytes_accessed=10**6, transcendentals=0),
        name=name,
    )(*operands)


def spread_kernel(keys, values, copies):
    for k in range(NZ):
        copies[k, :, 0:HEAD] = keys[...]
        copies[k, :, HEAD:2 * HEAD] = values[...]


def after_kernel(*refs):
    pass


def after(value, *others):
    anywhere = pl.BlockSpec(memory_space=pl.ANY)
    return pl.pallas_call(
        after_kernel,
        out_shape=jax.ShapeDtypeStruct(value.shape, value.dtype),
        in_specs=[anywhere] * (1 + len(others)),
        out_specs=anywhere,
        input_output_aliases={0: 0},
        name="after",
    )(value, *others)


def shift(value, axis, distance):
    size = lax.axis_size(axis)
    return lax.ppermute(value, axis, [(i, (i + distance) % size) for i in range(size)])


def wide(value):
    return value.astype(jnp.float32)


def shards(queries, keys, values, out_grad, out_weight, pair_order):
    table = tables(pair_order)
    bf16, f32 = jnp.bfloat16, jnp.float32

    parts = {k: shift(out_grad, "y", k) for k in (1, 3, 2)}
    copies = pl.pallas_call(
        spread_kernel,
        out_shape=jax.ShapeDtypeStruct((NZ, 2 * SPAN, 2 * HEAD), bf16),
        in_specs=[VMEM, VMEM],
        out_specs=VMEM,
        cost_estimate=pl.CostEstimate(flops=SPREAD_FLOPS, bytes_accessed=10**6, transcendentals=0),
        name="spread",
    )(keys, values)
    rows, columns = out_grad.shape
    heads = out_weight.shape[0]
    summed, rest = project_call(
        project_own_kernel, "project_own", [((heads, rows), f32), ((NY - 1, heads, columns), bf16)],
        3 * 10**8, [out_grad, out_weight], [copies],
    )
    near_queries = shift(queries, "x", 1)
    all_queries = [queries, near_queries, shift(near_queries, "x", 1), shift(queries, "x", 3)]
    (summed,) = project_call(
        project_near_kernel, "project_near", [((heads, rows), f32)], 6 * 10**8,
        [parts[1], parts[3], rest, summed],
    )
    (head_grads,) = project_call(
        project_far_kernel, "project_far", [((rows, heads), bf16)], 3 * 10**8,
        [parts[2], rest, summed], [table],
    )

    along_z = lax.all_to_all(copies, "z", 0, 0, tiled=True)
    marks = sum(array[:8, :HEAD] for array in (head_grads, *all_queries[1:]))
    along_z = after(along_z, marks)
    chunks = [along_z, shift(along_z, "c", 1)]

    kv, q_n, q_t, stats, o_t = kernel_call(
        forward_kernel, "forward",
        [((KEYS, 2 * HEAD), bf16), ((QSETS + 1, ROWS, HEAD), bf16), ((QSETS + 1, HEAD, ROWS), bf16),
         ((2, QSETS + 1, 8, ROWS), f32), ((QSETS + 1, HEAD, ROWS), f32)],
        [((QSETS + 1, 8, ROWS), f32)],
        4 * 10**9, table, *all_queries, *chunks,
    )
    all_grads = [head_grads] + [shift(head_grads, "x", k) for k in (1, 2, 3)]
    g_n, g_t, stats = kernel_call(
        weight_kernel, "weights",
        [((QSETS + 1, ROWS, HEAD), bf16), ((QSETS + 1, HEAD, ROWS), bf16), ((3, QSETS, ROWS), f32)],
        [], 10**7, table, *all_grads, stats, o_t,
    )
    all_stats = [stats] + [shift(stats, "x", k) for k in (1, 2, 3)]
    query_own, query_parts, terms = kernel_call(
        backward_kernel, "backward",
        [((2 * SPAN, HEADS * HEAD), f32), ((NX - 1, 2 * SPAN, HEADS * HEAD), bf16),
         ((KEY_DEVICES, 2 * SPAN, 2 * HEAD), bf16)],
        [((KEYS, 2 * HEAD), f32), ((QSETS + 1, HEAD, ROWS), f32), ((QSETS + 1, 8, ROWS), f32),
         ((QSETS + 1, 8, ROWS), f32)],
        8 * 10**9, table, *all_stats, kv, q_n, q_t, g_n, g_t,
    )
    query_gradient = query_own
    for k in (1, 2, 3):
        query_gradient = query_gradient + wide(shift(query_parts[k - 1], "x", k))

    terms = terms.reshape(NC, NZ, 2 * SPAN, 2 * HEAD)
    total = wide(terms[0]) + wide(shift(terms[1], "c", 1))
    total = lax.all_to_all(total.astype(bf16), "z", 0, 0, tiled=True)
    total = jnp.sum(wide(total), axis=0)
    return query_gradient, total[:, :HEAD], total[:, HEAD:]


def solution(mesh):
    split = Mesh(mesh.devices.reshape(NZ, NX, NC, NY), ("z", "x", "c", "y"))
    ctx = ("z", "x", "c")
    return jax.shard_map(
        shards,
        mesh=split,
        in_specs=(P(ctx, "y"), P(ctx, "y"), P(ctx, "y"), P(ctx, "y"), P("y", None), P()),
        out_specs=(P(ctx, "y"), P(ctx, "y"), P(ctx, "y")),
        check_vma=False,
    )
```

```python
import jax
import jax.numpy as jnp
from jax import lax
from jax.experimental import pallas as pl
from jax.experimental.pallas import tpu as pltpu
from jax.sharding import Mesh, PartitionSpec as P

HEAD = 128
HEADS = 6
SPAN = 64
SPANS = 128
ROWS = HEADS * SPAN
BLOCK = 256
PER_BLOCK = BLOCK // SPAN
LOG2E = 1.4426950408889634
SCALE = HEAD ** -0.5
NZ, NX, NC, NY = 8, 4, 2, 4
QSETS = 2 * NX
KEY_DEVICES = NZ * NC
KEY_SPANS = 2 * KEY_DEVICES
KEYS = KEY_SPANS * SPAN
MAX_STEPS = 48
T_RANK, T_SPAN, T_QSPAN, T_QSET, T_BLOCK, T_COUNT, T_X, T_C, T_FULL = (
    0, 16, 48, 64, 112, 160, 161, 162, 163
)
TABLE = 192
SPREAD_FLOPS = 2 * 10**10
LOW = -1e30
PAIR_STEPS = 6


def table_kernel(pair, table):
    z, x, c = lax.axis_index("z"), lax.axis_index("x"), lax.axis_index("c")
    keys = [pair[((i // NC) * NX + x) * NC + i % NC] for i in range(KEY_DEVICES)]
    ranks = [jnp.int32(0)] * KEY_DEVICES
    for i in range(KEY_DEVICES):
        for j in range(i):
            less = (keys[j] < keys[i]).astype(jnp.int32)
            ranks[i] = ranks[i] + less
            ranks[j] = ranks[j] + (1 - less)
    for i in range(KEY_DEVICES):
        table[T_RANK + i] = ranks[i]
        table[T_SPAN + ranks[i]] = keys[i]
        table[T_SPAN + KEY_SPANS - 1 - ranks[i]] = SPANS - 1 - keys[i]
    table[T_X] = x
    table[T_C] = c
    end = jnp.int32(0)
    lasts = []
    for u in range(QSETS):
        low = pair[(z * NX + u // 2) * NC + c]
        below = jnp.int32(0)
        same = jnp.int32(0)
        for key in keys:
            below = below + (key < low).astype(jnp.int32)
            same = same + (key == low).astype(jnp.int32)
        if u % 2 == 0:
            table[T_QSPAN + u] = low
            seen = below + same
        else:
            table[T_QSPAN + u] = SPANS - 1 - low
            seen = KEY_SPANS - below
        last = (seen + PER_BLOCK - 1) // PER_BLOCK - 1
        lasts.append(last)

        def fill(j, carry, u=u, end=end):
            table[T_QSET + end + j] = u
            table[T_BLOCK + end + j] = j
            return carry

        lax.fori_loop(0, last, fill, 0)
        end = end + jnp.maximum(last, 0)
    table[T_FULL] = end // PAIR_STEPS * PAIR_STEPS
    for u in range(QSETS):
        none = lasts[u] < 0
        table[T_QSET + end + u] = jnp.where(none, QSETS, u)
        table[T_BLOCK + end + u] = jnp.maximum(lasts[u], 0)
    table[T_COUNT] = end + QSETS
    table[T_QSPAN + QSETS] = -SPANS
    for k in range(PAIR_STEPS - 1):
        table[T_QSET + end + QSETS + k] = QSETS
        table[T_BLOCK + end + QSETS + k] = 0


def tables(pair_order):
    return pl.pallas_call(
        table_kernel,
        out_shape=jax.ShapeDtypeStruct((TABLE,), jnp.int32),
        in_specs=[SMEM],
        out_specs=SMEM,
        cost_estimate=pl.CostEstimate(flops=10**6, bytes_accessed=10**3, transcendentals=0),
        name="tables",
    )(pair_order)


def masked_scores(table, keys, q_t, u, j, masked):
    sc = jnp.dot(keys, q_t[u], preferred_element_type=jnp.float32)
    if not masked:
        return sc
    row = lax.broadcasted_iota(jnp.int32, (SPAN, ROWS), 0)
    col = lax.broadcasted_iota(jnp.int32, (SPAN, ROWS), 1) % SPAN
    ahead = row - col
    q_span = table[T_QSPAN + u]
    pieces = []
    for i in range(PER_BLOCK):
        room = (q_span - table[T_SPAN + j * PER_BLOCK + i]) * SPAN
        pieces.append(jnp.where(ahead <= room, sc[i * SPAN:(i + 1) * SPAN, :], -jnp.inf))
    return jnp.concatenate(pieces, axis=0)


def step_loops(table, body):
    full = table[T_FULL] // PAIR_STEPS
    end = (table[T_COUNT] + PAIR_STEPS - 1) // PAIR_STEPS
    lax.fori_loop(0, full, lambda i, carry: body(i, carry, False), 0)
    lax.fori_loop(full, end, lambda i, carry: body(i, carry, True), 0)


def block_rows(j):
    return pl.ds(pl.multiple_of(j * BLOCK, BLOCK), BLOCK)


def forward_kernel(table, *refs):
    queries = refs[:NX]
    own, other, kv, q_n, q_t, stats, o_t, m_s = refs[NX:]
    x = table[T_X]
    for i in range(KEY_DEVICES):
        dc, z = i // NZ, i % NZ
        chunk = (own, other)[dc]
        rank = table[T_RANK + z * NC + (table[T_C] + dc) % NC]
        for half, slot in ((0, rank), (1, KEY_SPANS - 1 - rank)):
            kv[pl.ds(pl.multiple_of(slot * SPAN, SPAN), SPAN), :] = (
                chunk[z, pl.ds(half * SPAN, SPAN), :]
            )
    for dx in range(NX):
        base = ((x + NX - dx) % NX) * 2
        for s in range(2):
            for h in range(HEADS):
                q_n[base + s, pl.ds(h * SPAN, SPAN), :] = (
                    queries[dx][pl.ds(s * SPAN, SPAN), pl.ds(h * HEAD, HEAD)]
                )
            q_t[base + s] = q_n[base + s].T
    q_t[QSETS] = jnp.zeros((HEAD, ROWS), jnp.bfloat16)
    o_t[...] = jnp.zeros_like(o_t)
    stats[1] = jnp.zeros((QSETS + 1, 8, ROWS), jnp.float32)
    m_s[...] = jnp.full_like(m_s, LOW)

    def body(i, carry, masked):
        us = [table[T_QSET + i * PAIR_STEPS + k] for k in range(PAIR_STEPS)]
        js = [table[T_BLOCK + i * PAIR_STEPS + k] for k in range(PAIR_STEPS)]
        scs = [masked_scores(table, kv[block_rows(j), 0:HEAD], q_t, u, j, masked) for u, j in zip(us, js)]
        tops = [jnp.max(sc, axis=0, keepdims=True) for sc in scs]
        for u, j, sc, top in zip(us, js, scs, tops):
            old = m_s[u]
            new = jnp.maximum(old, top)
            f = jnp.exp2((old - new) * (SCALE * LOG2E))
            e = jnp.exp2((sc - new[0:1, :]) * (SCALE * LOG2E))
            m_s[u] = new
            stats[1, u] = stats[1, u] * f + jnp.sum(e, axis=0, keepdims=True)
            o_t[u] = o_t[u] * f[0:1, :] + lax.dot_general(
                kv[block_rows(j), HEAD:2 * HEAD], e.astype(jnp.bfloat16),
                (((0,), (0,)), ((), ())), preferred_element_type=jnp.float32,
            )
        return carry

    step_loops(table, body)
    stats[0] = m_s[...]


def weight_kernel(table, *refs):
    grads = refs[:NX]
    stats, o_t = refs[NX:NX + 2]
    g_n, g_t, stats_out = refs[NX + 2:]
    x = table[T_X]
    for dx in range(NX):
        base = ((x + NX - dx) % NX) * 2
        for s in range(2):
            u = base + s
            for h in range(HEADS):
                g_n[u, pl.ds(h * SPAN, SPAN), :] = (
                    grads[dx][pl.ds(s * SPAN, SPAN), pl.ds(h * HEAD, HEAD)]
                )
            turned = g_n[u].T
            g_t[u] = turned
            w = jnp.sum(turned.astype(jnp.float32) * o_t[u], axis=0, keepdims=True)
            stats_out[2, pl.ds(u, 1), :] = w
            stats_out[0, pl.ds(u, 1), :] = stats[0, u, 0:1, :]
            stats_out[1, pl.ds(u, 1), :] = stats[1, u, 0:1, :]
    g_n[QSETS] = jnp.zeros((ROWS, HEAD), jnp.bfloat16)
    g_t[QSETS] = jnp.zeros((HEAD, ROWS), jnp.bfloat16)


def backward_kernel(table, *refs):
    stats = refs[:NX]
    kv, q_n, q_t, g_n, g_t, own_ref, part_ref, out_ref = refs[NX:NX + 8]
    acc, dq_t, lse_s, delta_s = refs[NX + 8:]
    x = table[T_X]
    top = stats[0][0]
    for r in stats[1:]:
        top = jnp.maximum(top, r[0])
    total = jnp.zeros((QSETS, ROWS), jnp.float32)
    weight = jnp.zeros((QSETS, ROWS), jnp.float32)
    for r in stats:
        f = jnp.exp2((r[0] - top) * (SCALE * LOG2E))
        total = total + r[1] * f
        weight = weight + r[2] * f
    lse = top * (SCALE * LOG2E) + jnp.log2(total)
    delta = weight / total
    for u in range(QSETS):
        lse_s[u] = jnp.broadcast_to(lse[u:u + 1, :], (8, ROWS))
        delta_s[u] = jnp.broadcast_to(delta[u:u + 1, :], (8, ROWS))
    lse_s[QSETS] = jnp.zeros((8, ROWS), jnp.float32)
    delta_s[QSETS] = jnp.zeros((8, ROWS), jnp.float32)
    acc[...] = jnp.zeros_like(acc)
    dq_t[...] = jnp.zeros_like(dq_t)

    def body(i, carry, masked):
        us = [table[T_QSET + i * PAIR_STEPS + k] for k in range(PAIR_STEPS)]
        js = [table[T_BLOCK + i * PAIR_STEPS + k] for k in range(PAIR_STEPS)]
        scs = [masked_scores(table, kv[block_rows(j), 0:HEAD], q_t, u, j, masked) for u, j in zip(us, js)]
        dps = [
            jnp.dot(kv[block_rows(j), HEAD:2 * HEAD], g_t[u], preferred_element_type=jnp.float32)
            for u, j in zip(us, js)
        ]
        for u, j, sc, dp in zip(us, js, scs, dps):
            p = jnp.exp2(sc * (SCALE * LOG2E) - lse_s[u][0:1, :])
            ds = (p * (dp - delta_s[u][0:1, :])).astype(jnp.bfloat16)
            rows = block_rows(j)
            acc[rows, HEAD:2 * HEAD] += jnp.dot(
                p.astype(jnp.bfloat16), g_n[u], preferred_element_type=jnp.float32
            )
            acc[rows, 0:HEAD] += jnp.dot(ds, q_n[u], preferred_element_type=jnp.float32)
            dq_t[u] += lax.dot_general(
                kv[rows, 0:HEAD], ds, (((0,), (0,)), ((), ())), preferred_element_type=jnp.float32
            )
        return carry

    step_loops(table, body)

    for i in range(KEY_DEVICES):
        rank = table[T_RANK + i]
        place = ((i + table[T_C]) % NC) * NZ + i // NC
        for half, slot in ((0, rank), (1, KEY_SPANS - 1 - rank)):
            rows = pl.ds(pl.multiple_of(slot * SPAN, SPAN), SPAN)
            out_ref[place, pl.ds(half * SPAN, SPAN), 0:HEAD] = (acc[rows, 0:HEAD] * SCALE).astype(jnp.bfloat16)
            out_ref[place, pl.ds(half * SPAN, SPAN), HEAD:2 * HEAD] = (
                acc[rows, HEAD:2 * HEAD].astype(jnp.bfloat16)
            )
    for dx in range(NX):
        base = ((x + dx) % NX) * 2
        for s in range(2):
            dq = dq_t[base + s].T * SCALE
            for h in range(HEADS):
                piece = dq[h * SPAN:(h + 1) * SPAN, :]
                rows, cols = pl.ds(s * SPAN, SPAN), pl.ds(h * HEAD, HEAD)
                if dx == 0:
                    own_ref[rows, cols] = piece
                else:
                    part_ref[dx - 1, rows, cols] = piece.astype(jnp.bfloat16)


def part_columns(k, columns):
    owner = (lax.axis_index("y") + NY - k) % NY
    return pl.ds(pl.multiple_of(owner * columns, columns), columns)


def weight_product(weight, part):
    return lax.dot_general(
        weight, part[...], (((1,), (1,)), ((), ())), preferred_element_type=jnp.float32
    )


def project_own_kernel(own, w_ref, unread, sum_ref, rest_ref):
    columns = own.shape[1]
    sum_ref[...] = weight_product(w_ref[:, part_columns(0, columns)], own)
    for k in range(1, NY):
        rest_ref[k - 1] = w_ref[:, part_columns(k, columns)]


def project_near_kernel(one, three, rest, sum_ref, out_ref):
    out_ref[...] = (
        sum_ref[...] + weight_product(rest[0], one) + weight_product(rest[2], three)
    )


def project_far_kernel(part, rest, sum_ref, *refs):
    out_ref = refs[-1]
    out_ref[...] = (sum_ref[...] + weight_product(rest[1], part)).T.astype(jnp.bfloat16)


def project_call(body, name, outs, flops, operands, unread=()):
    specs = [VMEM] * len(operands) + [pl.BlockSpec(memory_space=pl.ANY)] * len(unread)
    return pl.pallas_call(
        body,
        out_shape=tuple(jax.ShapeDtypeStruct(s, d) for s, d in outs),
        in_specs=specs,
        out_specs=tuple(VMEM for _ in outs),
        compiler_params=pltpu.CompilerParams(vmem_limit_bytes=24 * 1024 * 1024),
        cost_estimate=pl.CostEstimate(flops=flops, bytes_accessed=10**6, transcendentals=0),
        name=name,
    )(*operands, *unread)


SMEM = pl.BlockSpec(memory_space=pltpu.SMEM)
VMEM = pl.BlockSpec(memory_space=pltpu.VMEM)


def kernel_call(body, name, outs, scratch, flops, *operands):
    return pl.pallas_call(
        body,
        out_shape=tuple(jax.ShapeDtypeStruct(s, d) for s, d in outs),
        in_specs=[SMEM] + [VMEM] * (len(operands) - 1),
        out_specs=tuple(VMEM for _ in outs),
        scratch_shapes=[pltpu.VMEM(s, d) for s, d in scratch],
        compiler_params=pltpu.CompilerParams(vmem_limit_bytes=40 * 1024 * 1024),
        cost_estimate=pl.CostEstimate(flops=flops, bytes_accessed=10**6, transcendentals=0),
        name=name,
    )(*operands)


def spread_kernel(keys, values, copies):
    for k in range(NZ):
        copies[k, :, 0:HEAD] = keys[...]
        copies[k, :, HEAD:2 * HEAD] = values[...]


def after_kernel(*refs):
    pass


def after(value, *others):
    anywhere = pl.BlockSpec(memory_space=pl.ANY)
    return pl.pallas_call(
        after_kernel,
        out_shape=jax.ShapeDtypeStruct(value.shape, value.dtype),
        in_specs=[anywhere] * (1 + len(others)),
        out_specs=anywhere,
        input_output_aliases={0: 0},
        name="after",
    )(value, *others)


def shift(value, axis, distance):
    size = lax.axis_size(axis)
    return lax.ppermute(value, axis, [(i, (i + distance) % size) for i in range(size)])


def wide(value):
    return value.astype(jnp.float32)


def shards(queries, keys, values, out_grad, out_weight, pair_order):
    table = tables(pair_order)
    bf16, f32 = jnp.bfloat16, jnp.float32

    parts = {k: shift(out_grad, "y", k) for k in (1, 3, 2)}
    copies = pl.pallas_call(
        spread_kernel,
        out_shape=jax.ShapeDtypeStruct((NZ, 2 * SPAN, 2 * HEAD), bf16),
        in_specs=[VMEM, VMEM],
        out_specs=VMEM,
        cost_estimate=pl.CostEstimate(flops=SPREAD_FLOPS, bytes_accessed=10**6, transcendentals=0),
        name="spread",
    )(keys, values)
    rows, columns = out_grad.shape
    heads = out_weight.shape[0]
    summed, rest = project_call(
        project_own_kernel, "project_own", [((heads, rows), f32), ((NY - 1, heads, columns), bf16)],
        3 * 10**8, [out_grad, out_weight], [copies],
    )
    near_queries = shift(queries, "x", 1)
    all_queries = [queries, near_queries, shift(near_queries, "x", 1), shift(queries, "x", 3)]
    (summed,) = project_call(
        project_near_kernel, "project_near", [((heads, rows), f32)], 6 * 10**8,
        [parts[1], parts[3], rest, summed],
    )
    (head_grads,) = project_call(
        project_far_kernel, "project_far", [((rows, heads), bf16)], 3 * 10**8,
        [parts[2], rest, summed], [table],
    )

    along_z = lax.all_to_all(copies, "z", 0, 0, tiled=True)
    marks = sum(array[:8, :HEAD] for array in (head_grads, *all_queries[1:]))
    along_z = after(along_z, marks)
    chunks = [along_z, shift(along_z, "c", 1)]

    kv, q_n, q_t, stats, o_t = kernel_call(
        forward_kernel, "forward",
        [((KEYS, 2 * HEAD), bf16), ((QSETS + 1, ROWS, HEAD), bf16), ((QSETS + 1, HEAD, ROWS), bf16),
         ((2, QSETS + 1, 8, ROWS), f32), ((QSETS + 1, HEAD, ROWS), f32)],
        [((QSETS + 1, 8, ROWS), f32)],
        4 * 10**9, table, *all_queries, *chunks,
    )
    all_grads = [head_grads] + [shift(head_grads, "x", k) for k in (1, 2, 3)]
    g_n, g_t, stats = kernel_call(
        weight_kernel, "weights",
        [((QSETS + 1, ROWS, HEAD), bf16), ((QSETS + 1, HEAD, ROWS), bf16), ((3, QSETS, ROWS), f32)],
        [], 10**7, table, *all_grads, stats, o_t,
    )
    all_stats = [stats] + [shift(stats, "x", k) for k in (1, 2, 3)]
    query_own, query_parts, terms = kernel_call(
        backward_kernel, "backward",
        [((2 * SPAN, HEADS * HEAD), f32), ((NX - 1, 2 * SPAN, HEADS * HEAD), bf16),
         ((KEY_DEVICES, 2 * SPAN, 2 * HEAD), bf16)],
        [((KEYS, 2 * HEAD), f32), ((QSETS + 1, HEAD, ROWS), f32), ((QSETS + 1, 8, ROWS), f32),
         ((QSETS + 1, 8, ROWS), f32)],
        8 * 10**9, table, *all_stats, kv, q_n, q_t, g_n, g_t,
    )
    query_gradient = query_own
    for k in (1, 2, 3):
        query_gradient = query_gradient + wide(shift(query_parts[k - 1], "x", k))

    terms = terms.reshape(NC, NZ, 2 * SPAN, 2 * HEAD)
    total = wide(terms[0]) + wide(shift(terms[1], "c", 1))
    total = lax.all_to_all(total.astype(bf16), "z", 0, 0, tiled=True)
    total = jnp.sum(wide(total), axis=0)
    return query_gradient, total[:, :HEAD], total[:, HEAD:]


def solution(mesh):
    split = Mesh(mesh.devices.reshape(NZ, NX, NC, NY), ("z", "x", "c", "y"))
    ctx = ("z", "x", "c")
    return jax.shard_map(
        shards,
        mesh=split,
        in_specs=(P(ctx, "y"), P(ctx, "y"), P(ctx, "y"), P(ctx, "y"), P("y", None), P()),
        out_specs=(P(ctx, "y"), P(ctx, "y"), P(ctx, "y")),
        check_vma=False,
    )
```
